32 devices in a mesh: groups: 2 (over y), seq: 4 (over z), dp: 4 (over x, core).
Axes of the slice: x: 2, y: 2, z: 4, core: 2. Of those that a mesh axis runs over, the one named last changes fastest.
Arguments:
- inputs: bfloat16 [8, 4096, 448], P(('groups', 'dp'), 'seq'), parts along dimension 0, may hold values from -6 to 6
- cotangent: bfloat16 [8, 4096, 448], P(('groups', 'dp'), 'seq'), parts along dimension 0, may hold values from -6 to 6
- first_weight_matrix: bfloat16 [3, 448, 448], P(None, None, 'dp'), may hold values from -0.15625 to 0.15625
- weight_two: bfloat16 [3, 448, 448], P(None, None, 'dp'), may hold values from -0.15625 to 0.15625
Outputs:
- input_grad: bfloat16 [8, 4096, 448], P(('groups', 'dp'), 'seq'), parts along dimension 0
- grad_one: float32 [6, 448, 448], P('groups', None, 'dp'), parts along dimension 0
- grad_two: float32 [6, 448, 448], P('groups', None, 'dp'), parts along dimension 0
The draws below stay inside these ranges and needn't reach their ends.
There are 2 independent parts, one for each index of `groups`. The reference program is written for one: setup_inputs(seed, part) draws one part's arguments, and reference() takes and returns one part's arrays. A program takes and returns all parts, laid end to end along the dimension named above; an argument that names none is the same for every part. Nothing has to cross between parts.
All inputs are finite; a program needn't handle non-finite values.
Results may differ from the reference program's by a relative error of at most 0.012.
Values may be sent and summed in bfloat16 or wider, within the bound.
A program may use at most 64 MiB of HBM per device.

```python
import math
import jax
import jax.numpy as jnp
from jax import lax

C = 448
POS_DEV = 1024
SEQS = 4
LEN = 4096
FIRST_SPACING = 2048
SECOND_SPACING = 4096
N_SEQ = 4


def spiked(drawn, own_key, source, target, parts, factor):
    owner, partner = [(jnp.arange(drawn.shape[axis_at]) // (drawn.shape[axis_at] // parts)).reshape([-1 if axis == axis_at else 1 for axis in range(drawn.ndim)]) for axis_at in (source, target)]
    chosen = jax.random.permutation(own_key, parts)[partner]
    strong = (owner == chosen) | (owner == (partner + parts // 2) % parts)
    return jnp.where(strong, factor * drawn, drawn)


def level_of(stream_key, shape, cuts, low, top_value):
    gain = 1.0
    for axis_at, parts in cuts:
        draws = jax.random.uniform(jax.random.fold_in(jax.random.fold_in(stream_key, 6), axis_at), (parts,), jnp.float32, low / len(cuts), top_value / len(cuts))
        gain = gain * jnp.repeat(jnp.exp(draws), shape[axis_at] // parts).reshape((-1,) + (1,) * (len(shape) - 1 - axis_at))
    return gain


def normal_values(own_key, dims, scale, bound, split=(), held_as=jnp.bfloat16):
    array = scale * jax.random.normal(own_key, dims, jnp.float32)
    if split:
        array = array * level_of(own_key, dims, split, -0.22, 0.18)
    return jnp.clip(array, -bound, bound).astype(held_as)


def bell_draw_with(rng, shape, spread, limit, cuts, heavy, held_as=jnp.bfloat16):
    drawn = spread * jax.random.normal(rng, shape, jnp.float32)
    if cuts:
        drawn = drawn * level_of(rng, shape, cuts, -0.22, 0.18)
    return jnp.clip(spiked(drawn, jax.random.fold_in(rng, 3), *heavy), -limit, limit).astype(held_as)


def setup_inputs(seed: int = 0, part: int = 0) -> dict:
    key_of = jax.random.split(jax.random.key(seed), 5)
    part_keys = jax.random.split(jax.random.fold_in(key_of[4], part), 5)
    return {
        "inputs": normal_values(part_keys[0], (SEQS, LEN, C), 1.0, 6.0, ((0, 4), (1, 4))),
        "cotangent": bell_draw_with(part_keys[1], (SEQS, LEN, C), 1.0, 6.0, ((0, 4), (1, 4)), (0, 2, 4, 2.0)),
        "first_weight_matrix": normal_values(key_of[2], (3, C, C), (3 * C) ** -0.5, 0.15625, ((2, 4),)),
        "weight_two": normal_values(key_of[3], (3, C, C), (3 * C) ** -0.5, 0.15625, ((2, 4),)),
    }


def gelu_slope(value):
    return jax.vjp(jax.nn.gelu, value)[1](jnp.ones_like(value))[0]

def displaced_rows(values, offset):
    count = values.shape[0]
    if offset >= count or -offset >= count:
        return jnp.zeros_like(values)
    filler = jnp.zeros((abs(offset), values.shape[1]), values.dtype)
    if offset > 0:
        return jnp.concatenate([filler, values[:count - offset]], axis=0)
    return jnp.concatenate([values[-offset:], filler], axis=0)

def block_terms(left, right, factor):
    left_blocks = left.reshape(N_SEQ, POS_DEV, C).astype(jnp.float32)
    right_blocks = right.reshape(N_SEQ, POS_DEV, C).astype(jnp.float32)
    terms = jnp.einsum('bpc,bpd->bcd', left_blocks, right_blocks) * factor
    rounded = lax.optimization_barrier(terms.astype(jnp.bfloat16))
    return lax.optimization_barrier(jnp.sum(rounded.astype(jnp.float32), axis=0))

def one_sequence(inputs, cotangent, first_weight_matrix, weight_two, factor):
    input_activation = jax.nn.gelu(inputs.astype(jnp.float32)).astype(jnp.bfloat16)
    preactivation = jnp.dot(displaced_rows(input_activation, FIRST_SPACING), first_weight_matrix[0], preferred_element_type=jnp.float32)
    preactivation = preactivation + jnp.dot(input_activation, first_weight_matrix[1], preferred_element_type=jnp.float32)
    preactivation = preactivation + jnp.dot(displaced_rows(input_activation, -FIRST_SPACING), first_weight_matrix[2], preferred_element_type=jnp.float32)
    hidden_f = (inputs.astype(jnp.float32) + preactivation).astype(jnp.bfloat16).astype(jnp.float32)
    act_one = jax.nn.gelu(hidden_f).astype(jnp.bfloat16)
    second_layer_taps = [displaced_rows(cotangent, -SECOND_SPACING), cotangent, displaced_rows(cotangent, SECOND_SPACING)]
    delta_one = jnp.zeros(inputs.shape, jnp.float32)
    for k in range(3):
        delta_one = delta_one + jnp.dot(second_layer_taps[k], weight_two[k].T, preferred_element_type=jnp.float32)
    middle_gradient = (cotangent.astype(jnp.float32) + gelu_slope(hidden_f) * delta_one).astype(jnp.bfloat16)
    first_layer_taps = [displaced_rows(middle_gradient, -FIRST_SPACING), middle_gradient, displaced_rows(middle_gradient, FIRST_SPACING)]
    delta_zero = jnp.zeros(inputs.shape, jnp.float32)
    for k in range(3):
        delta_zero = delta_zero + jnp.dot(first_layer_taps[k], first_weight_matrix[k].T, preferred_element_type=jnp.float32)
    inputs_f = inputs.astype(jnp.float32)
    input_grad = (middle_gradient.astype(jnp.float32) + gelu_slope(inputs_f) * delta_zero).astype(jnp.bfloat16)
    grad_two = jnp.stack([block_terms(act_one, second_layer_taps[k], factor) for k in range(3)])
    grad_one = jnp.stack([block_terms(input_activation, first_layer_taps[k], factor) for k in range(3)])
    return (input_grad, grad_one, grad_two)

def reference(inputs, cotangent, first_weight_matrix, weight_two):
    factor = 1.0 / math.sqrt(SEQS * LEN)

    def run(pair):
        return one_sequence(pair[0], pair[1], first_weight_matrix, weight_two, factor)
    input_grad, grad_one, grad_two = lax.map(run, (inputs, cotangent))
    return (input_grad, lax.optimization_barrier(jnp.sum(grad_one, axis=0)), lax.optimization_barrier(jnp.sum(grad_two, axis=0)))
```

```python
import functools
import math

import jax
import jax.numpy as jnp
from jax import lax
from jax.experimental import pallas as pl
from jax.experimental.pallas import tpu as pltpu
from jax.sharding import PartitionSpec as P


MESH = pl.DeviceIdType.MESH
FIRST_SPACING = 2048
SECOND_SPACING = 4096
CHUNKS = 4


def shifted(block, axis, distance):
    devices = range(lax.axis_size(axis))
    route = [(i - distance, i) for i in devices if i - distance in devices]
    return lax.ppermute(block, axis, route)


def gelu_slope(value):
    return jax.vjp(jax.nn.gelu, value)[1](jnp.ones_like(value))[0]


def outer_terms(left, right, factor):
    product = lax.dot_general(
        left, right, (((0,), (0,)), ((), ())), preferred_element_type=jnp.float32
    )
    return product * factor


def back_product(tap, weight):
    return lax.dot_general(
        tap, weight, (((1,), (1,)), ((), ())), preferred_element_type=jnp.float32
    )


def spread_plan(inputs, cotangent, first_weight_matrix, weight_two):
    chans = inputs.shape[2]
    rows = inputs.shape[0] * inputs.shape[1]
    factor = 1.0 / math.sqrt(
        inputs.shape[0] * lax.axis_size("dp") * inputs.shape[1] * lax.axis_size("seq")
    )
    full_one = lax.all_gather(first_weight_matrix, "dp", axis=2, tiled=True)
    flat_in = inputs.reshape(rows, chans)
    inputs_f = flat_in.astype(jnp.float32)
    input_activation = jax.nn.gelu(inputs_f).astype(jnp.bfloat16)
    act_before = shifted(input_activation, "seq", 2)
    act_after = shifted(input_activation, "seq", -2)
    flat_cot = cotangent.reshape(rows, chans)
    cot_later = shifted(flat_cot, "seq", -4)
    cot_earlier = shifted(flat_cot, "seq", 4)
    preactivation = jnp.dot(act_before, full_one[0], preferred_element_type=jnp.float32)
    preactivation = preactivation + jnp.dot(
        input_activation, full_one[1], preferred_element_type=jnp.float32
    )
    preactivation = preactivation + jnp.dot(
        act_after, full_one[2], preferred_element_type=jnp.float32
    )
    hidden_f = (inputs_f + preactivation).astype(jnp.bfloat16).astype(jnp.float32)
    act_one = jax.nn.gelu(hidden_f).astype(jnp.bfloat16)
    full_two = lax.all_gather(weight_two, "dp", axis=2, tiled=True)
    second_layer_taps = (cot_later, flat_cot, cot_earlier)
    delta_one = back_product(second_layer_taps[0], full_two[0])
    delta_one = delta_one + back_product(second_layer_taps[1], full_two[1])
    delta_one = delta_one + back_product(second_layer_taps[2], full_two[2])
    middle_gradient = (flat_cot.astype(jnp.float32) + gelu_slope(hidden_f) * delta_one).astype(
        jnp.bfloat16
    )
    part_two = jnp.stack(
        [outer_terms(act_one, second_layer_taps[k], factor) for k in range(3)]
    ).astype(jnp.bfloat16)
    grad_two = lax.psum(
        lax.psum_scatter(part_two, "dp", scatter_dimension=2, tiled=True).astype(jnp.float32), "seq"
    )
    grad_later = shifted(middle_gradient, "seq", -2)
    grad_earlier = shifted(middle_gradient, "seq", 2)
    first_layer_taps = (grad_later, middle_gradient, grad_earlier)
    delta_zero = back_product(first_layer_taps[0], full_one[0])
    delta_zero = delta_zero + back_product(first_layer_taps[1], full_one[1])
    delta_zero = delta_zero + back_product(first_layer_taps[2], full_one[2])
    input_grad = (middle_gradient.astype(jnp.float32) + gelu_slope(inputs_f) * delta_zero).astype(
        jnp.bfloat16
    )
    part_one = jnp.stack(
        [outer_terms(input_activation, first_layer_taps[k], factor) for k in range(3)]
    ).astype(jnp.bfloat16)
    grad_one = lax.psum(
        lax.psum_scatter(part_one, "dp", scatter_dimension=2, tiled=True).astype(jnp.float32), "seq"
    )
    return (input_grad.reshape(inputs.shape), grad_one, grad_two)


def pack(left, right):
    cut = right.shape[1] // 128 * 128
    return jnp.concatenate([left, right[:, cut:], right[:, :cut]], axis=1)


def unpack(both):
    chans = both.shape[1] // 2
    rest = chans % 128
    right = jnp.concatenate([both[:, chans + rest :], both[:, chans : chans + rest]], axis=1)
    return both[:, :chans], right


def gelu_and_slope(value):
    inner = math.sqrt(2.0 / math.pi)
    square = value * value
    bend = jnp.tanh(inner * value * (1.0 + 0.044715 * square))
    half = 0.5 * (1.0 + bend)
    slope = half + 0.5 * value * (1.0 - bend * bend) * (inner * (1.0 + 3.0 * 0.044715 * square))
    return value * half, slope


def forward(rows, weight_t):
    return lax.dot_general(
        rows, weight_t, (((1,), (1,)), ((), ())), preferred_element_type=jnp.float32
    )


def backward(rows, weight_t):
    return jnp.dot(rows, weight_t, preferred_element_type=jnp.float32)


def outer(left, right):
    return lax.dot_general(
        left, right, (((0,), (0,)), ((), ())), preferred_element_type=jnp.float32
    )


def pair_kernel(
    factor,
    x_ref, c_ref, w1_ref, w2_ref,
    ig_ref, gr_ref,
    sendb, xs, retb, retr, igs, wts, wt, terms,
    s_core, r_core, s_chip, r_chip, acc, s_near, r_near, s_far, r_far, s_last, r_last,
    xs_send, xs_recv, ret_send, ret_recv, w_send, w_recv, red_send, red_recv,
):
    f32, bf16 = jnp.float32, jnp.bfloat16
    chans = x_ref.shape[1]
    half = x_ref.shape[0] // 2
    rows = half // CHUNKS
    width = wts.shape[1]
    z, d = lax.axis_index("seq"), lax.axis_index("dp")
    role = z // 2
    other = 1 - role
    far = lax.rem(z + 2, 4)
    parity = lax.rem(z, 2)
    near = z + 1 - 2 * parity
    core = lax.rem(d, 2)
    chip = d // 2
    sibling = d + 1 - 2 * core
    across = lax.rem(d + 2, 4)

    barrier = pltpu.get_barrier_semaphore()
    for j in (1, 2, 3):
        pl.semaphore_signal(
            barrier, inc=1, device_id={"dp": lax.rem(d + j, 4)}, device_id_type=MESH
        )
    for peer in (near, far):
        pl.semaphore_signal(barrier, inc=1, device_id={"seq": peer}, device_id_type=MESH)

    def at_rows(start, size):
        return pl.ds(pl.multiple_of(start, 16), size)

    def move(ch):
        piece = at_rows(ch * rows, rows)
        return pltpu.make_async_remote_copy(
            src_ref=sendb.at[piece],
            dst_ref=xs.at[role, piece],
            send_sem=xs_send.at[ch],
            recv_sem=xs_recv.at[ch],
            device_id={"seq": far},
            device_id_type=MESH,
        )

    def give_back(ch):
        piece = at_rows(ch * (rows // 2), rows // 2)
        return pltpu.make_async_remote_copy(
            src_ref=retb.at[piece],
            dst_ref=retr.at[piece],
            send_sem=ret_send.at[ch],
            recv_sem=ret_recv.at[ch],
            device_id={"seq": far},
            device_id_type=MESH,
        )

    def pack_chunk(ch, carry):
        from_rows = at_rows(other * half + ch * rows, rows)
        sendb[at_rows(ch * rows, rows), :] = pack(x_ref[from_rows, :], c_ref[from_rows, :])
        return carry

    lax.fori_loop(0, CHUNKS, pack_chunk, 0)
    pl.semaphore_wait(barrier, 5)
    for ch in range(CHUNKS):
        move(ch).start()

    taps = (w1_ref.at[0], w1_ref.at[1], w1_ref.at[2], w2_ref.at[1])
    mine = at_rows(d * width, width)
    for k, tap in enumerate(taps):
        turned = tap[...].astype(f32).T.astype(bf16)
        wts[k] = turned
        wt[k, mine, :] = turned

    def share(j):
        return pltpu.make_async_remote_copy(
            src_ref=wts,
            dst_ref=wt.at[:, mine],
            send_sem=w_send.at[j - 1],
            recv_sem=w_recv.at[j - 1],
            device_id={"dp": lax.rem(d + j, 4)},
            device_id_type=MESH,
        )

    for j in (1, 2, 3):
        share(j).start()

    def keep_chunk(ch, carry):
        from_rows = at_rows(role * half + ch * rows, rows)
        xs[role, at_rows(ch * rows, rows), :] = pack(x_ref[from_rows, :], c_ref[from_rows, :])
        return carry

    lax.fori_loop(0, CHUNKS, keep_chunk, 0)
    terms[...] = jnp.zeros_like(terms)
    for j in (1, 2, 3):
        share(j).wait()

    def work(ch, carry):
        move(ch).wait_recv()

        @pl.when(ch == CHUNKS - 1)
        def _():
            for early in range(CHUNKS - 1):
                give_back(early).start()

        piece = at_rows(ch * rows, rows)
        both = xs[:, piece, :].reshape(2 * rows, 2 * chans)
        x_b, c_b = unpack(both)
        x_f = x_b.astype(f32)
        act, slope_x = gelu_and_slope(x_f)
        act = act.astype(bf16)
        cross = jnp.concatenate([forward(act[rows:], wt[2]), forward(act[:rows], wt[0])], axis=0)
        hidden = (x_f + (forward(act, wt[1]) + cross)).astype(bf16).astype(f32)
        act_one, slope_h = gelu_and_slope(hidden)
        act_one = act_one.astype(bf16)
        grad_mid = (c_b.astype(f32) + slope_h * backward(c_b, wt[3])).astype(bf16)
        cross = jnp.concatenate(
            [backward(grad_mid[rows:], wt[0]), backward(grad_mid[:rows], wt[2])], axis=0
        )
        delta = backward(grad_mid, wt[1]) + cross
        result = (grad_mid.astype(f32) + slope_x * delta).astype(bf16)
        igs[...] = result.reshape(2, rows, chans)
        terms[3] += outer(c_b, act_one)
        terms[0] += outer(grad_mid[rows:], act[:rows])
        terms[1] += outer(grad_mid, act)
        terms[2] += outer(grad_mid[:rows], act[rows:])
        ig_ref[at_rows(role * half + ch * rows, rows), :] = igs[role]
        back = igs[other]
        retb[at_rows(ch * (rows // 2), rows // 2), :] = pack(back[: rows // 2], back[rows // 2 :])
        return carry

    lax.fori_loop(0, CHUNKS, work, 0)
    give_back(CHUNKS - 1).start()

    def slice_of(owner):
        owned = at_rows(owner * width, width)
        own = [terms[k, owned, :] * factor for k in range(4)]
        return pack(own[0], own[1]), pack(own[2], own[3])

    def reduce_copy(index, src, dst, axis, peer):
        return pltpu.make_async_remote_copy(
            src_ref=src,
            dst_ref=dst,
            send_sem=red_send.at[index],
            recv_sem=red_recv.at[index],
            device_id={axis: peer},
            device_id_type=MESH,
        )

    to_core = []
    for j, for_chip in enumerate((1 - chip, chip)):
        first, second = slice_of(2 * for_chip + 1 - core)
        s_core[j, 0] = first.astype(bf16)
        s_core[j, 1] = second.astype(bf16)
        to_core.append(reduce_copy(j, s_core.at[j], r_core.at[j], "dp", sibling))
        to_core[j].start()
    to_core[0].wait_recv()
    for p, part in enumerate(slice_of(2 * (1 - chip) + core)):
        s_chip[p] = (part + r_core[0, p].astype(f32)).astype(bf16)
    to_chip = reduce_copy(2, s_chip, r_chip, "dp", across)
    to_chip.start()
    to_core[1].wait_recv()
    for p, part in enumerate(slice_of(d)):
        acc[p] = part + r_core[1, p].astype(f32)
    to_chip.wait_recv()
    for p in range(2):
        acc[p] += r_chip[p].astype(f32)

    s_near[...] = acc[1 - parity].astype(bf16)
    to_near = reduce_copy(3, s_near, r_near, "seq", near)
    to_near.start()
    to_near.wait_recv()
    s_far[...] = (acc[parity] + r_near[...].astype(f32)).astype(bf16)
    to_far = reduce_copy(4, s_far, r_far, "seq", far)
    to_far.start()

    for ch in range(CHUNKS):
        give_back(ch).wait_recv()
        left, right = unpack(retr[ch * (rows // 2) : (ch + 1) * (rows // 2), :])
        at = other * half + ch * rows
        ig_ref[at_rows(at, rows // 2), :] = left
        ig_ref[at_rows(at + rows // 2, rows // 2), :] = right

    to_far.wait_recv()
    s_last[...] = (s_far[...].astype(f32) + r_far[...].astype(f32)).astype(bf16)
    to_last = reduce_copy(5, s_last, r_last, "seq", near)
    to_last.start()
    gr_ref[parity] = s_last[...].astype(f32)
    to_last.wait_recv()
    gr_ref[1 - parity] = r_last[...].astype(f32)

    for ch in range(CHUNKS):
        move(ch).wait_send()
        give_back(ch).wait_send()
    for copy in (*to_core, to_chip, to_near, to_far, to_last):
        copy.wait_send()


def pair_plan(inputs, cotangent, first_weight_matrix, weight_two):
    positions, chans = inputs.shape[1:]
    width = first_weight_matrix.shape[2]
    factor = 1.0 / math.sqrt(
        lax.axis_size("dp") * positions * lax.axis_size("seq")
    )
    half = positions // 2
    f32, bf16 = jnp.float32, jnp.bfloat16
    vmem = pl.BlockSpec(memory_space=pltpu.VMEM)
    dma = pltpu.SemaphoreType.DMA
    packed = (width, 2 * chans)
    result, sums = pl.pallas_call(
        functools.partial(pair_kernel, factor),
        out_shape=(
            jax.ShapeDtypeStruct((positions, chans), bf16),
            jax.ShapeDtypeStruct((2, *packed), f32),
        ),
        in_specs=[vmem] * 4,
        out_specs=(vmem, vmem),
        scratch_shapes=[
            pltpu.VMEM((half, 2 * chans), bf16),
            pltpu.VMEM((2, half, 2 * chans), bf16),
            pltpu.VMEM((half // 2, 2 * chans), bf16),
            pltpu.VMEM((half // 2, 2 * chans), bf16),
            pltpu.VMEM((2, half // CHUNKS, chans), bf16),
            pltpu.VMEM((4, width, chans), bf16),
            pltpu.VMEM((4, chans, chans), bf16),
            pltpu.VMEM((4, chans, chans), f32),
            pltpu.VMEM((2, 2, *packed), bf16),
            pltpu.VMEM((2, 2, *packed), bf16),
            pltpu.VMEM((2, *packed), bf16),
            pltpu.VMEM((2, *packed), bf16),
            pltpu.VMEM((2, *packed), f32),
            *[pltpu.VMEM(packed, bf16)] * 6,
            dma((CHUNKS,)), dma((CHUNKS,)), dma((CHUNKS,)), dma((CHUNKS,)),
            dma((3,)), dma((3,)), dma((6,)), dma((6,)),
        ],
        compiler_params=pltpu.CompilerParams(
            collective_id=0, has_side_effects=True, vmem_limit_bytes=48 * 2**20
        ),
    )(inputs[0], cotangent[0], first_weight_matrix, weight_two)
    pair_one = unpack(sums[0])
    pair_two = unpack(sums[1])
    grad_one = jnp.stack([pair_one[0].T, pair_one[1].T, pair_two[0].T])
    middle = pair_two[1].T
    outside = jnp.zeros_like(middle)
    grad_two = jnp.stack([outside, middle, outside])
    return result[None], grad_one, grad_two


def on_device(inputs, cotangent, first_weight_matrix, weight_two):
    sequences, positions, chans = inputs.shape
    length = positions * lax.axis_size("seq")
    paired = lax.axis_size("seq") == 4 and lax.axis_size("dp") == 4 and sequences == 1
    if paired and length == 2 * FIRST_SPACING and length <= SECOND_SPACING:
        return pair_plan(inputs, cotangent, first_weight_matrix, weight_two)
    return spread_plan(inputs, cotangent, first_weight_matrix, weight_two)


def solution(mesh):
    placed = (
        P(("groups", "dp"), "seq", None),
        P(("groups", "dp"), "seq", None),
        P(None, None, "dp"),
        P(None, None, "dp"),
    )
    return jax.shard_map(
        on_device,
        mesh=mesh,
        in_specs=placed,
        out_specs=(
            P(("groups", "dp"), "seq", None),
            P("groups", None, "dp"),
            P("groups", None, "dp"),
        ),
        check_vma=False,
    )
```

```python
import functools
import math

import jax
import jax.numpy as jnp
from jax import lax
from jax.experimental import pallas as pl
from jax.experimental.pallas import tpu as pltpu
from jax.sharding import PartitionSpec as P


MESH = pl.DeviceIdType.MESH
FIRST_SPACING = 2048
SECOND_SPACING = 4096
CHUNKS = 4
AHEAD = 2


def shifted(block, axis, distance):
    devices = range(lax.axis_size(axis))
    route = [(i - distance, i) for i in devices if i - distance in devices]
    return lax.ppermute(block, axis, route)


def gelu_slope(value):
    return jax.vjp(jax.nn.gelu, value)[1](jnp.ones_like(value))[0]


def outer_terms(left, right, factor):
    product = lax.dot_general(
        left, right, (((0,), (0,)), ((), ())), preferred_element_type=jnp.float32
    )
    return product * factor


def back_product(tap, weight):
    return lax.dot_general(
        tap, weight, (((1,), (1,)), ((), ())), preferred_element_type=jnp.float32
    )


def spread_plan(inputs, cotangent, first_weight_matrix, weight_two):
    chans = inputs.shape[2]
    rows = inputs.shape[0] * inputs.shape[1]
    factor = 1.0 / math.sqrt(
        inputs.shape[0] * lax.axis_size("dp") * inputs.shape[1] * lax.axis_size("seq")
    )
    full_one = lax.all_gather(first_weight_matrix, "dp", axis=2, tiled=True)
    flat_in = inputs.reshape(rows, chans)
    inputs_f = flat_in.astype(jnp.float32)
    input_activation = jax.nn.gelu(inputs_f).astype(jnp.bfloat16)
    act_before = shifted(input_activation, "seq", 2)
    act_after = shifted(input_activation, "seq", -2)
    flat_cot = cotangent.reshape(rows, chans)
    cot_later = shifted(flat_cot, "seq", -4)
    cot_earlier = shifted(flat_cot, "seq", 4)
    preactivation = jnp.dot(act_before, full_one[0], preferred_element_type=jnp.float32)
    preactivation = preactivation + jnp.dot(
        input_activation, full_one[1], preferred_element_type=jnp.float32
    )
    preactivation = preactivation + jnp.dot(
        act_after, full_one[2], preferred_element_type=jnp.float32
    )
    hidden_f = (inputs_f + preactivation).astype(jnp.bfloat16).astype(jnp.float32)
    act_one = jax.nn.gelu(hidden_f).astype(jnp.bfloat16)
    full_two = lax.all_gather(weight_two, "dp", axis=2, tiled=True)
    second_layer_taps = (cot_later, flat_cot, cot_earlier)
    delta_one = back_product(second_layer_taps[0], full_two[0])
    delta_one = delta_one + back_product(second_layer_taps[1], full_two[1])
    delta_one = delta_one + back_product(second_layer_taps[2], full_two[2])
    middle_gradient = (flat_cot.astype(jnp.float32) + gelu_slope(hidden_f) * delta_one).astype(
        jnp.bfloat16
    )
    part_two = jnp.stack(
        [outer_terms(act_one, second_layer_taps[k], factor) for k in range(3)]
    ).astype(jnp.bfloat16)
    grad_two = lax.psum(
        lax.psum_scatter(part_two, "dp", scatter_dimension=2, tiled=True).astype(jnp.float32), "seq"
    )
    grad_later = shifted(middle_gradient, "seq", -2)
    grad_earlier = shifted(middle_gradient, "seq", 2)
    first_layer_taps = (grad_later, middle_gradient, grad_earlier)
    delta_zero = back_product(first_layer_taps[0], full_one[0])
    delta_zero = delta_zero + back_product(first_layer_taps[1], full_one[1])
    delta_zero = delta_zero + back_product(first_layer_taps[2], full_one[2])
    input_grad = (middle_gradient.astype(jnp.float32) + gelu_slope(inputs_f) * delta_zero).astype(
        jnp.bfloat16
    )
    part_one = jnp.stack(
        [outer_terms(input_activation, first_layer_taps[k], factor) for k in range(3)]
    ).astype(jnp.bfloat16)
    grad_one = lax.psum(
        lax.psum_scatter(part_one, "dp", scatter_dimension=2, tiled=True).astype(jnp.float32), "seq"
    )
    return (input_grad.reshape(inputs.shape), grad_one, grad_two)


def pack(left, right):
    cut = right.shape[1] // 128 * 128
    return jnp.concatenate([left, right[:, cut:], right[:, :cut]], axis=1)


def unpack(both):
    chans = both.shape[1] // 2
    rest = chans % 128
    right = jnp.concatenate([both[:, chans + rest :], both[:, chans : chans + rest]], axis=1)
    return both[:, :chans], right


def gelu_and_slope(value):
    inner = math.sqrt(2.0 / math.pi)
    square = value * value
    bend = jnp.tanh(inner * value * (1.0 + 0.044715 * square))
    half = 0.5 * (1.0 + bend)
    slope = half + 0.5 * value * (1.0 - bend * bend) * (inner * (1.0 + 3.0 * 0.044715 * square))
    return value * half, slope


def product(left, right):
    return jnp.dot(left, right, preferred_element_type=jnp.float32)


def outer(left, right):
    return lax.dot_general(
        left, right, (((1,), (1,)), ((), ())), preferred_element_type=jnp.float32
    )


def pair_kernel(
    factor,
    x_ref, c_ref, w1_ref, w2_ref,
    ig_ref, gr_ref,
    xs, retb, igs, taps, wts, wt, wn, terms,
    s_core, r_core, s_chip, r_chip, acc, s_near, r_near, s_far, r_far, s_last, r_last,
    xs_send, xs_recv, own_sem, tap_sem, ret_send, ret_recv, w_send, w_recv, red_send, red_recv,
):
    f32, bf16 = jnp.float32, jnp.bfloat16
    chans, positions = x_ref.shape
    half = positions // 2
    size = half // CHUNKS
    width = wts.shape[1]
    z, d = lax.axis_index("seq"), lax.axis_index("dp")
    role = z // 2
    other = 1 - role
    far = lax.rem(z + 2, 4)
    parity = lax.rem(z, 2)
    near = z + 1 - 2 * parity
    core = lax.rem(d, 2)
    chip = d // 2
    sibling = d + 1 - 2 * core
    across = lax.rem(d + 2, 4)

    barrier = pltpu.get_barrier_semaphore()
    for axis, peer in (("seq", far), ("seq", near), ("dp", sibling), ("dp", across)):
        pl.semaphore_signal(barrier, inc=1, device_id={axis: peer}, device_id_type=MESH)

    own_half = pl.ds(pl.multiple_of(role * half, 128), half)
    own_copies = [
        pltpu.make_async_copy(ref.at[:, own_half], xs.at[role, i], own_sem.at[i])
        for i, ref in enumerate((x_ref, c_ref))
    ]
    tap_copies = [
        pltpu.make_async_copy(w1_ref, taps.at[pl.ds(0, 3)], tap_sem.at[0]),
        pltpu.make_async_copy(w2_ref.at[1], taps.at[3], tap_sem.at[1]),
    ]

    def columns(start, count):
        return pl.ds(pl.multiple_of(start, 128), count)

    def owned_rows(owner):
        return pl.ds(pl.multiple_of(owner * width, 16), width)

    def remote(src, dst, send, recv, axis, peer):
        return pltpu.make_async_remote_copy(
            src_ref=src, dst_ref=dst, send_sem=send, recv_sem=recv,
            device_id={axis: peer}, device_id_type=MESH,
        )

    def move(ch):
        return [
            remote(
                ref.at[:, columns(other * half + ch * size, size)],
                xs.at[role, i, :, columns(ch * size, size)],
                xs_send.at[ch, i], xs_recv.at[ch, i], "seq", far,
            )
            for i, ref in enumerate((x_ref, c_ref))
        ]

    def give_back(ch):
        return remote(
            retb.at[:, columns(ch * size, size)],
            ig_ref.at[:, columns(role * half + ch * size, size)],
            ret_send.at[ch], ret_recv.at[ch], "seq", far,
        )

    for copy in tap_copies:
        copy.start()
    pl.semaphore_wait(barrier, 4)
    for ch in range(AHEAD):
        for copy in move(ch):
            copy.start()
    for copy in own_copies:
        copy.start()

    for copy in tap_copies:
        copy.wait()
    for k in range(4):
        turned = taps[k].astype(f32).T.astype(bf16)
        wts[k] = turned
        wt[k, owned_rows(d), :] = turned
    shares = [
        remote(
            wts, wt.at[:, owned_rows(d)], w_send.at[j], w_recv.at[j], "dp", peer
        )
        for j, peer in enumerate((across, sibling))
    ]
    for copy in shares:
        copy.start()
    terms[...] = jnp.zeros_like(terms)
    shares[0].wait_recv()
    arrived = wt.at[:, owned_rows(across)]
    passed = remote(arrived, arrived, w_send.at[2], w_recv.at[2], "dp", sibling)
    passed.start()
    shares[1].wait_recv()
    passed.wait_recv()
    for k in range(4):
        wn[k] = wt[k].astype(f32).T.astype(bf16)
    for copy in own_copies:
        copy.wait()

    def work(ch, carry):
        for copy in move(ch):
            copy.wait_recv()

        @pl.when(ch + AHEAD < CHUNKS)
        def _():
            for copy in move(ch + AHEAD):
                copy.start()

        @pl.when(ch == CHUNKS - 1)
        def _():
            for early in range(CHUNKS - 1):
                give_back(early).start()

        piece = columns(ch * size, size)
        x_f = jnp.concatenate([xs[0, 0, :, piece], xs[1, 0, :, piece]], axis=1).astype(f32)
        c_b = jnp.concatenate([xs[0, 1, :, piece], xs[1, 1, :, piece]], axis=1)
        act, slope_x = gelu_and_slope(x_f)
        act = act.astype(bf16)
        low, high = act[:, :size], act[:, size:]
        cross = jnp.concatenate([product(wt[2], high), product(wt[0], low)], axis=1)
        hidden = (x_f + (product(wt[1], act) + cross)).astype(bf16).astype(f32)
        act_one, slope_h = gelu_and_slope(hidden)
        act_one = act_one.astype(bf16)
        grad_mid = (c_b.astype(f32) + slope_h * product(wn[3], c_b)).astype(bf16)
        g_low, g_high = grad_mid[:, :size], grad_mid[:, size:]
        terms[3] += outer(c_b, act_one)
        terms[0] += outer(g_high, low)
        terms[1] += outer(grad_mid, act)
        terms[2] += outer(g_low, high)
        cross = jnp.concatenate([product(wn[0], g_high), product(wn[2], g_low)], axis=1)
        delta = product(wn[1], grad_mid) + cross
        result = (grad_mid.astype(f32) + slope_x * delta).astype(bf16)
        igs[0] = result[:, :size]
        igs[1] = result[:, size:]
        ig_ref[:, columns(role * half + ch * size, size)] = igs[role]
        retb[:, piece] = igs[other]
        return carry

    lax.fori_loop(0, CHUNKS, work, 0)
    give_back(CHUNKS - 1).start()

    steps = [(0, 48), (48, 32), (80, 32)] if width == 112 else [(0, width)]

    def slice_of(owner, start, count):
        owned = pl.ds(pl.multiple_of(owner * width + start, 16), count)
        own = [terms[k, owned, :] * factor for k in range(4)]
        return pack(own[0], own[1]), pack(own[2], own[3])

    def reduce_copy(kind, q, src, dst, axis, peer):
        return remote(src, dst, red_send.at[kind, q], red_recv.at[kind, q], axis, peer)

    copies = [[], [], [], [], [], []]
    for j, for_chip in enumerate((1 - chip, chip)):
        for q, (start, count) in enumerate(steps):
            span = pl.ds(start, count)
            for p, part in enumerate(slice_of(2 * for_chip + 1 - core, start, count)):
                s_core[j, p, span, :] = part.astype(bf16)
            copies[j].append(
                reduce_copy(
                    j, q, s_core.at[j, :, span], r_core.at[j, :, span], "dp", sibling
                )
            )
            copies[j][q].start()
    for q, (start, count) in enumerate(steps):
        span = pl.ds(start, count)
        copies[0][q].wait_recv()
        for p, part in enumerate(slice_of(2 * (1 - chip) + core, start, count)):
            s_chip[p, span, :] = (part + r_core[0, p, span, :].astype(f32)).astype(bf16)
        copies[2].append(
            reduce_copy(2, q, s_chip.at[:, span], r_chip.at[:, span], "dp", across)
        )
        copies[2][q].start()
    for q, (start, count) in enumerate(steps):
        span = pl.ds(start, count)
        copies[1][q].wait_recv()
        for p, part in enumerate(slice_of(d, start, count)):
            acc[p, span, :] = part + r_core[1, p, span, :].astype(f32)
    for q, (start, count) in enumerate(steps):
        span = pl.ds(start, count)
        copies[2][q].wait_recv()
        for p in range(2):
            acc[p, span, :] += r_chip[p, span, :].astype(f32)
        s_near[span, :] = acc[1 - parity, span, :].astype(bf16)
        copies[3].append(reduce_copy(3, q, s_near.at[span], r_near.at[span], "seq", near))
        copies[3][q].start()
    for q, (start, count) in enumerate(steps):
        span = pl.ds(start, count)
        copies[3][q].wait_recv()
        s_far[span, :] = (acc[parity, span, :] + r_near[span, :].astype(f32)).astype(bf16)
        copies[4].append(reduce_copy(4, q, s_far.at[span], r_far.at[span], "seq", far))
        copies[4][q].start()
    for q, (start, count) in enumerate(steps):
        span = pl.ds(start, count)
        copies[4][q].wait_recv()
        total = (s_far[span, :].astype(f32) + r_far[span, :].astype(f32)).astype(bf16)
        s_last[span, :] = total
        copies[5].append(reduce_copy(5, q, s_last.at[span], r_last.at[span], "seq", near))
        copies[5][q].start()
        for i, part in enumerate(unpack(total.astype(f32))):
            gr_ref[2 * parity + i, span, :] = part
    for q, (start, count) in enumerate(steps):
        span = pl.ds(start, count)
        copies[5][q].wait_recv()
        for i, part in enumerate(unpack(r_last[span, :].astype(f32))):
            gr_ref[2 * (1 - parity) + i, span, :] = part

    for ch in range(CHUNKS):
        give_back(ch).wait()
        for copy in move(ch):
            copy.wait_send()
    for group in (shares, [passed], *copies):
        for copy in group:
            copy.wait_send()


def pair_plan(inputs, cotangent, first_weight_matrix, weight_two):
    positions, chans = inputs.shape[1:]
    width = first_weight_matrix.shape[2]
    factor = 1.0 / math.sqrt(
        lax.axis_size("dp") * positions * lax.axis_size("seq")
    )
    half = positions // 2
    f32, bf16 = jnp.float32, jnp.bfloat16
    vmem = pl.BlockSpec(memory_space=pltpu.VMEM)
    hbm = pl.BlockSpec(memory_space=pltpu.HBM)
    dma = pltpu.SemaphoreType.DMA
    packed = (width, 2 * chans)
    result, sums = pl.pallas_call(
        functools.partial(pair_kernel, factor),
        out_shape=(
            jax.ShapeDtypeStruct((chans, positions), bf16),
            jax.ShapeDtypeStruct((4, width, chans), f32),
        ),
        in_specs=[hbm] * 4,
        out_specs=(vmem, vmem),
        scratch_shapes=[
            pltpu.VMEM((2, 2, chans, half), bf16),
            pltpu.VMEM((chans, half), bf16),
            pltpu.VMEM((2, chans, half // CHUNKS), bf16),
            pltpu.VMEM((4, chans, width), bf16),
            pltpu.VMEM((4, width, chans), bf16),
            pltpu.VMEM((4, chans, chans), bf16),
            pltpu.VMEM((4, chans, chans), bf16),
            pltpu.VMEM((4, chans, chans), f32),
            pltpu.VMEM((2, 2, *packed), bf16),
            pltpu.VMEM((2, 2, *packed), bf16),
            pltpu.VMEM((2, *packed), bf16),
            pltpu.VMEM((2, *packed), bf16),
            pltpu.VMEM((2, *packed), f32),
            *[pltpu.VMEM(packed, bf16)] * 6,
            dma((CHUNKS, 2)), dma((CHUNKS, 2)), dma((2,)), dma((2,)),
            dma((CHUNKS,)), dma((CHUNKS,)), dma((3,)), dma((3,)), dma((6, 3)), dma((6, 3)),
        ],
        compiler_params=pltpu.CompilerParams(
            collective_id=0, has_side_effects=True, vmem_limit_bytes=62 * 2**20
        ),
    )(inputs[0].T, cotangent[0].T, first_weight_matrix, weight_two)
    sums = sums.transpose(0, 2, 1)
    return result.T[None], sums[:3], jnp.pad(sums[3:], ((1, 1), (0, 0), (0, 0)))


def on_device(inputs, cotangent, first_weight_matrix, weight_two):
    sequences, positions, chans = inputs.shape
    length = positions * lax.axis_size("seq")
    paired = lax.axis_size("seq") == 4 and lax.axis_size("dp") == 4 and sequences == 1
    if paired and length == 2 * FIRST_SPACING and length <= SECOND_SPACING:
        return pair_plan(inputs, cotangent, first_weight_matrix, weight_two)
    return spread_plan(inputs, cotangent, first_weight_matrix, weight_two)


def solution(mesh):
    placed = (
        P(("groups", "dp"), "seq", None),
        P(("groups", "dp"), "seq", None),
        P(None, None, "dp"),
        P(None, None, "dp"),
    )
    return jax.shard_map(
        on_device,
        mesh=mesh,
        in_specs=placed,
        out_specs=(
            P(("groups", "dp"), "seq", None),
            P("groups", None, "dp"),
            P("groups", None, "dp"),
        ),
        check_vma=False,
    )
```

```python
import functools
import math

import jax
import jax.numpy as jnp
from jax import lax
from jax.experimental import pallas as pl
from jax.experimental.pallas import tpu as pltpu
from jax.sharding import PartitionSpec as P


MESH = pl.DeviceIdType.MESH
FIRST_SPACING = 2048
SECOND_SPACING = 4096
CHUNKS = 4
AHEAD = 2


def shifted(block, axis, distance):
    devices = range(lax.axis_size(axis))
    route = [(i - distance, i) for i in devices if i - distance in devices]
    return lax.ppermute(block, axis, route)


def gelu_slope(value):
    return jax.vjp(jax.nn.gelu, value)[1](jnp.ones_like(value))[0]


def outer_terms(left, right, factor):
    product = lax.dot_general(
        left, right, (((0,), (0,)), ((), ())), preferred_element_type=jnp.float32
    )
    return product * factor


def back_product(tap, weight):
    return lax.dot_general(
        tap, weight, (((1,), (1,)), ((), ())), preferred_element_type=jnp.float32
    )


def spread_plan(inputs, cotangent, first_weight_matrix, weight_two):
    chans = inputs.shape[2]
    rows = inputs.shape[0] * inputs.shape[1]
    factor = 1.0 / math.sqrt(
        inputs.shape[0] * lax.axis_size("dp") * inputs.shape[1] * lax.axis_size("seq")
    )
    full_one = lax.all_gather(first_weight_matrix, "dp", axis=2, tiled=True)
    flat_in = inputs.reshape(rows, chans)
    inputs_f = flat_in.astype(jnp.float32)
    input_activation = jax.nn.gelu(inputs_f).astype(jnp.bfloat16)
    act_before = shifted(input_activation, "seq", 2)
    act_after = shifted(input_activation, "seq", -2)
    flat_cot = cotangent.reshape(rows, chans)
    cot_later = shifted(flat_cot, "seq", -4)
    cot_earlier = shifted(flat_cot, "seq", 4)
    preactivation = jnp.dot(act_before, full_one[0], preferred_element_type=jnp.float32)
    preactivation = preactivation + jnp.dot(
        input_activation, full_one[1], preferred_element_type=jnp.float32
    )
    preactivation = preactivation + jnp.dot(
        act_after, full_one[2], preferred_element_type=jnp.float32
    )
    hidden_f = (inputs_f + preactivation).astype(jnp.bfloat16).astype(jnp.float32)
    act_one = jax.nn.gelu(hidden_f).astype(jnp.bfloat16)
    full_two = lax.all_gather(weight_two, "dp", axis=2, tiled=True)
    second_layer_taps = (cot_later, flat_cot, cot_earlier)
    delta_one = back_product(second_layer_taps[0], full_two[0])
    delta_one = delta_one + back_product(second_layer_taps[1], full_two[1])
    delta_one = delta_one + back_product(second_layer_taps[2], full_two[2])
    middle_gradient = (flat_cot.astype(jnp.float32) + gelu_slope(hidden_f) * delta_one).astype(
        jnp.bfloat16
    )
    part_two = jnp.stack(
        [outer_terms(act_one, second_layer_taps[k], factor) for k in range(3)]
    ).astype(jnp.bfloat16)
    grad_two = lax.psum(
        lax.psum_scatter(part_two, "dp", scatter_dimension=2, tiled=True).astype(jnp.float32), "seq"
    )
    grad_later = shifted(middle_gradient, "seq", -2)
    grad_earlier = shifted(middle_gradient, "seq", 2)
    first_layer_taps = (grad_later, middle_gradient, grad_earlier)
    delta_zero = back_product(first_layer_taps[0], full_one[0])
    delta_zero = delta_zero + back_product(first_layer_taps[1], full_one[1])
    delta_zero = delta_zero + back_product(first_layer_taps[2], full_one[2])
    input_grad = (middle_gradient.astype(jnp.float32) + gelu_slope(inputs_f) * delta_zero).astype(
        jnp.bfloat16
    )
    part_one = jnp.stack(
        [outer_terms(input_activation, first_layer_taps[k], factor) for k in range(3)]
    ).astype(jnp.bfloat16)
    grad_one = lax.psum(
        lax.psum_scatter(part_one, "dp", scatter_dimension=2, tiled=True).astype(jnp.float32), "seq"
    )
    return (input_grad.reshape(inputs.shape), grad_one, grad_two)


def pack(left, right):
    cut = right.shape[1] // 128 * 128
    return jnp.concatenate([left, right[:, cut:], right[:, :cut]], axis=1)


def unpack(both):
    chans = both.shape[1] // 2
    rest = chans % 128
    right = jnp.concatenate([both[:, chans + rest :], both[:, chans : chans + rest]], axis=1)
    return both[:, :chans], right


def gelu_and_slope(value):
    inner = math.sqrt(2.0 / math.pi)
    square = value * value
    bend = jnp.tanh(inner * value * (1.0 + 0.044715 * square))
    half = 0.5 * (1.0 + bend)
    slope = half + 0.5 * value * (1.0 - bend * bend) * (inner * (1.0 + 3.0 * 0.044715 * square))
    return value * half, slope


def product(left, right):
    return jnp.dot(left, right, preferred_element_type=jnp.float32)


def outer(left, right):
    return lax.dot_general(
        left, right, (((1,), (1,)), ((), ())), preferred_element_type=jnp.float32
    )


def pair_kernel(
    factor,
    x_ref, c_ref, w1_ref, w2_ref,
    ig_ref, g_one_ref, g_two_ref,
    sums, xs, retb, igs, taps, wts, wt, wn, terms,
    s_core, r_core, s_chip, r_chip, acc, s_near, r_near, s_far, r_far, s_last, r_last,
    xs_send, xs_recv, own_sem, tap_sem, ret_send, ret_recv, w_send, w_recv, red_send, red_recv,
):
    f32, bf16 = jnp.float32, jnp.bfloat16
    chans, positions = x_ref.shape
    half = positions // 2
    size = half // CHUNKS
    width = wts.shape[1]
    z, d = lax.axis_index("seq"), lax.axis_index("dp")
    role = z // 2
    other = 1 - role
    far = lax.rem(z + 2, 4)
    parity = lax.rem(z, 2)
    near = z + 1 - 2 * parity
    core = lax.rem(d, 2)
    chip = d // 2
    sibling = d + 1 - 2 * core
    across = lax.rem(d + 2, 4)

    barrier = pltpu.get_barrier_semaphore()
    for axis, peer in (("seq", far), ("seq", near), ("dp", sibling), ("dp", across)):
        pl.semaphore_signal(barrier, inc=1, device_id={axis: peer}, device_id_type=MESH)

    own_half = pl.ds(pl.multiple_of(role * half, 128), half)
    own_copies = [
        pltpu.make_async_copy(ref.at[:, own_half], xs.at[role, i], own_sem.at[i])
        for i, ref in enumerate((x_ref, c_ref))
    ]
    tap_copies = [
        pltpu.make_async_copy(w1_ref, taps.at[pl.ds(0, 3)], tap_sem.at[0]),
        pltpu.make_async_copy(w2_ref.at[1], taps.at[3], tap_sem.at[1]),
    ]

    def columns(start, count):
        return pl.ds(pl.multiple_of(start, 128), count)

    def owned_rows(owner):
        return pl.ds(pl.multiple_of(owner * width, 16), width)

    def remote(src, dst, send, recv, axis, peer):
        return pltpu.make_async_remote_copy(
            src_ref=src, dst_ref=dst, send_sem=send, recv_sem=recv,
            device_id={axis: peer}, device_id_type=MESH,
        )

    def move(ch):
        return [
            remote(
                ref.at[:, columns(other * half + ch * size, size)],
                xs.at[role, i, :, columns(ch * size, size)],
                xs_send.at[ch, i], xs_recv.at[ch, i], "seq", far,
            )
            for i, ref in enumerate((x_ref, c_ref))
        ]

    def give_back(ch):
        return remote(
            retb.at[:, columns(ch * size, size)],
            ig_ref.at[:, columns(role * half + ch * size, size)],
            ret_send.at[ch], ret_recv.at[ch], "seq", far,
        )

    for copy in tap_copies:
        copy.start()
    pl.semaphore_wait(barrier, 4)
    for ch in range(AHEAD):
        for copy in move(ch):
            copy.start()
    for copy in own_copies:
        copy.start()

    for copy in tap_copies:
        copy.wait()
    for k in range(4):
        turned = taps[k].astype(f32).T.astype(bf16)
        wts[k] = turned
        wt[k, owned_rows(d), :] = turned
    shares = [
        remote(
            wts, wt.at[:, owned_rows(d)], w_send.at[j], w_recv.at[j], "dp", peer
        )
        for j, peer in enumerate((across, sibling))
    ]
    for copy in shares:
        copy.start()
    terms[...] = jnp.zeros_like(terms)
    shares[0].wait_recv()
    arrived = wt.at[:, owned_rows(across)]
    passed = remote(arrived, arrived, w_send.at[2], w_recv.at[2], "dp", sibling)
    passed.start()
    shares[1].wait_recv()
    passed.wait_recv()
    for k in range(4):
        wn[k] = wt[k].astype(f32).T.astype(bf16)
    for copy in own_copies:
        copy.wait()

    def work(ch, carry):
        for copy in move(ch):
            copy.wait_recv()

        @pl.when(ch + AHEAD < CHUNKS)
        def _():
            for copy in move(ch + AHEAD):
                copy.start()

        @pl.when(ch == CHUNKS - 1)
        def _():
            for early in range(CHUNKS - 1):
                give_back(early).start()

        piece = columns(ch * size, size)
        x_f = jnp.concatenate([xs[0, 0, :, piece], xs[1, 0, :, piece]], axis=1).astype(f32)
        c_b = jnp.concatenate([xs[0, 1, :, piece], xs[1, 1, :, piece]], axis=1)
        act, slope_x = gelu_and_slope(x_f)
        act = act.astype(bf16)
        low, high = act[:, :size], act[:, size:]
        cross = jnp.concatenate([product(wt[2], high), product(wt[0], low)], axis=1)
        hidden = (x_f + (product(wt[1], act) + cross)).astype(bf16).astype(f32)
        act_one, slope_h = gelu_and_slope(hidden)
        act_one = act_one.astype(bf16)
        grad_mid = (c_b.astype(f32) + slope_h * product(wn[3], c_b)).astype(bf16)
        g_low, g_high = grad_mid[:, :size], grad_mid[:, size:]
        terms[3] += outer(c_b, act_one)
        terms[0] += outer(g_high, low)
        terms[1] += outer(grad_mid, act)
        terms[2] += outer(g_low, high)
        cross = jnp.concatenate([product(wn[0], g_high), product(wn[2], g_low)], axis=1)
        delta = product(wn[1], grad_mid) + cross
        result = (grad_mid.astype(f32) + slope_x * delta).astype(bf16)
        igs[0] = result[:, :size]
        igs[1] = result[:, size:]
        ig_ref[:, columns(role * half + ch * size, size)] = igs[role]
        retb[:, piece] = igs[other]
        return carry

    lax.fori_loop(0, CHUNKS, work, 0)

    steps = [(0, 48), (48, 32), (80, 32)] if width == 112 else [(0, width)]

    def slice_of(owner, start, count):
        owned = pl.ds(pl.multiple_of(owner * width + start, 16), count)
        own = [terms[k, owned, :] * factor for k in range(4)]
        return pack(own[0], own[1]), pack(own[2], own[3])

    def reduce_copy(kind, q, src, dst, axis, peer):
        return remote(src, dst, red_send.at[kind, q], red_recv.at[kind, q], axis, peer)

    copies = [[], [], [], [], [], []]
    for j, for_chip in enumerate((1 - chip, chip)):
        for q, (start, count) in enumerate(steps):
            span = pl.ds(start, count)
            for p, part in enumerate(slice_of(2 * for_chip + 1 - core, start, count)):
                s_core[j, p, span, :] = part.astype(bf16)
            copies[j].append(
                reduce_copy(
                    j, q, s_core.at[j, :, span], r_core.at[j, :, span], "dp", sibling
                )
            )
            copies[j][q].start()
    for q, (start, count) in enumerate(steps):
        span = pl.ds(start, count)
        copies[0][q].wait_recv()
        for p, part in enumerate(slice_of(2 * (1 - chip) + core, start, count)):
            s_chip[p, span, :] = (part + r_core[0, p, span, :].astype(f32)).astype(bf16)
        copies[2].append(
            reduce_copy(2, q, s_chip.at[:, span], r_chip.at[:, span], "dp", across)
        )
        copies[2][q].start()
    for q, (start, count) in enumerate(steps):
        span = pl.ds(start, count)
        copies[1][q].wait_recv()
        for p, part in enumerate(slice_of(d, start, count)):
            acc[p, span, :] = part + r_core[1, p, span, :].astype(f32)
    for q, (start, count) in enumerate(steps):
        span = pl.ds(start, count)
        copies[2][q].wait_recv()
        for p in range(2):
            acc[p, span, :] += r_chip[p, span, :].astype(f32)
        s_near[span, :] = acc[1 - parity, span, :].astype(bf16)
        copies[3].append(reduce_copy(3, q, s_near.at[span], r_near.at[span], "seq", near))
        copies[3][q].start()
    for q, (start, count) in enumerate(steps):
        span = pl.ds(start, count)
        copies[3][q].wait_recv()
        s_far[span, :] = (acc[parity, span, :] + r_near[span, :].astype(f32)).astype(bf16)
        copies[4].append(reduce_copy(4, q, s_far.at[span], r_far.at[span], "seq", far))
        copies[4][q].start()
    give_back(CHUNKS - 1).start()
    outside = jnp.zeros((width, chans), f32)
    g_two_ref[0] = outside
    g_two_ref[2] = outside
    for q, (start, count) in enumerate(steps):
        span = pl.ds(start, count)
        copies[4][q].wait_recv()
        total = (s_far[span, :].astype(f32) + r_far[span, :].astype(f32)).astype(bf16)
        s_last[span, :] = total
        copies[5].append(reduce_copy(5, q, s_last.at[span], r_last.at[span], "seq", near))
        copies[5][q].start()
        for i, part in enumerate(unpack(total.astype(f32))):
            sums[2 * parity + i, span, :] = part
    for q, (start, count) in enumerate(steps):
        span = pl.ds(start, count)
        copies[5][q].wait_recv()
        for i, part in enumerate(unpack(r_last[span, :].astype(f32))):
            sums[2 * (1 - parity) + i, span, :] = part
        for k in range(3):
            g_one_ref[k, span, :] = sums[k, span, :]
        g_two_ref[1, span, :] = sums[3, span, :]

    for ch in range(CHUNKS):
        give_back(ch).wait()
        for copy in move(ch):
            copy.wait_send()
    for group in (shares, [passed], *copies):
        for copy in group:
            copy.wait_send()


def pair_plan(inputs, cotangent, first_weight_matrix, weight_two):
    positions, chans = inputs.shape[1:]
    width = first_weight_matrix.shape[2]
    factor = 1.0 / math.sqrt(
        lax.axis_size("dp") * positions * lax.axis_size("seq")
    )
    half = positions // 2
    f32, bf16 = jnp.float32, jnp.bfloat16
    vmem = pl.BlockSpec(memory_space=pltpu.VMEM)
    hbm = pl.BlockSpec(memory_space=pltpu.HBM)
    dma = pltpu.SemaphoreType.DMA
    packed = (width, 2 * chans)
    result, grad_one, grad_two = pl.pallas_call(
        functools.partial(pair_kernel, factor),
        out_shape=(
            jax.ShapeDtypeStruct((chans, positions), bf16),
            jax.ShapeDtypeStruct((3, width, chans), f32),
            jax.ShapeDtypeStruct((3, width, chans), f32),
        ),
        in_specs=[hbm] * 4,
        out_specs=(vmem, vmem, vmem),
        scratch_shapes=[
            pltpu.VMEM((4, width, chans), f32),
            pltpu.VMEM((2, 2, chans, half), bf16),
            pltpu.VMEM((chans, half), bf16),
            pltpu.VMEM((2, chans, half // CHUNKS), bf16),
            pltpu.VMEM((4, chans, width), bf16),
            pltpu.VMEM((4, width, chans), bf16),
            pltpu.VMEM((4, chans, chans), bf16),
            pltpu.VMEM((4, chans, chans), bf16),
            pltpu.VMEM((4, chans, chans), f32),
            pltpu.VMEM((2, 2, *packed), bf16),
            pltpu.VMEM((2, 2, *packed), bf16),
            pltpu.VMEM((2, *packed), bf16),
            pltpu.VMEM((2, *packed), bf16),
            pltpu.VMEM((2, *packed), f32),
            *[pltpu.VMEM(packed, bf16)] * 6,
            dma((CHUNKS, 2)), dma((CHUNKS, 2)), dma((2,)), dma((2,)),
            dma((CHUNKS,)), dma((CHUNKS,)), dma((3,)), dma((3,)), dma((6, 3)), dma((6, 3)),
        ],
        compiler_params=pltpu.CompilerParams(
            collective_id=0, has_side_effects=True, vmem_limit_bytes=62 * 2**20
        ),
    )(inputs[0].T, cotangent[0].T, first_weight_matrix, weight_two)
    return result.T[None], grad_one.transpose(0, 2, 1), grad_two.transpose(0, 2, 1)


def on_device(inputs, cotangent, first_weight_matrix, weight_two):
    sequences, positions, chans = inputs.shape
    length = positions * lax.axis_size("seq")
    paired = lax.axis_size("seq") == 4 and lax.axis_size("dp") == 4 and sequences == 1
    if paired and length == 2 * FIRST_SPACING and length <= SECOND_SPACING:
        return pair_plan(inputs, cotangent, first_weight_matrix, weight_two)
    return spread_plan(inputs, cotangent, first_weight_matrix, weight_two)


def solution(mesh):
    placed = (
        P(("groups", "dp"), "seq", None),
        P(("groups", "dp"), "seq", None),
        P(None, None, "dp"),
        P(None, None, "dp"),
    )
    return jax.shard_map(
        on_device,
        mesh=mesh,
        in_specs=placed,
        out_specs=(
            P(("groups", "dp"), "seq", None),
            P("groups", None, "dp"),
            P("groups", None, "dp"),
        ),
        check_vma=False,
    )
```

```python
import functools
import math

import jax
import jax.numpy as jnp
from jax import lax
from jax.experimental import pallas as pl
from jax.experimental.pallas import tpu as pltpu
from jax.sharding import PartitionSpec as P


MESH = pl.DeviceIdType.MESH
FIRST_SPACING = 2048
SECOND_SPACING = 4096
CHUNKS = 4
AHEAD = 3


def shifted(block, axis, distance):
    devices = range(lax.axis_size(axis))
    route = [(i - distance, i) for i in devices if i - distance in devices]
    return lax.ppermute(block, axis, route)


def gelu_slope(value):
    return jax.vjp(jax.nn.gelu, value)[1](jnp.ones_like(value))[0]


def outer_terms(left, right, factor):
    product = lax.dot_general(
        left, right, (((0,), (0,)), ((), ())), preferred_element_type=jnp.float32
    )
    return product * factor


def back_product(tap, weight):
    return lax.dot_general(
        tap, weight, (((1,), (1,)), ((), ())), preferred_element_type=jnp.float32
    )


def spread_plan(inputs, cotangent, first_weight_matrix, weight_two):
    chans = inputs.shape[2]
    rows = inputs.shape[0] * inputs.shape[1]
    factor = 1.0 / math.sqrt(
        inputs.shape[0] * lax.axis_size("dp") * inputs.shape[1] * lax.axis_size("seq")
    )
    full_one = lax.all_gather(first_weight_matrix, "dp", axis=2, tiled=True)
    flat_in = inputs.reshape(rows, chans)
    inputs_f = flat_in.astype(jnp.float32)
    input_activation = jax.nn.gelu(inputs_f).astype(jnp.bfloat16)
    act_before = shifted(input_activation, "seq", 2)
    act_after = shifted(input_activation, "seq", -2)
    flat_cot = cotangent.reshape(rows, chans)
    cot_later = shifted(flat_cot, "seq", -4)
    cot_earlier = shifted(flat_cot, "seq", 4)
    preactivation = jnp.dot(act_before, full_one[0], preferred_element_type=jnp.float32)
    preactivation = preactivation + jnp.dot(
        input_activation, full_one[1], preferred_element_type=jnp.float32
    )
    preactivation = preactivation + jnp.dot(
        act_after, full_one[2], preferred_element_type=jnp.float32
    )
    hidden_f = (inputs_f + preactivation).astype(jnp.bfloat16).astype(jnp.float32)
    act_one = jax.nn.gelu(hidden_f).astype(jnp.bfloat16)
    full_two = lax.all_gather(weight_two, "dp", axis=2, tiled=True)
    second_layer_taps = (cot_later, flat_cot, cot_earlier)
    delta_one = back_product(second_layer_taps[0], full_two[0])
    delta_one = delta_one + back_product(second_layer_taps[1], full_two[1])
    delta_one = delta_one + back_product(second_layer_taps[2], full_two[2])
    middle_gradient = (flat_cot.astype(jnp.float32) + gelu_slope(hidden_f) * delta_one).astype(
        jnp.bfloat16
    )
    part_two = jnp.stack(
        [outer_terms(act_one, second_layer_taps[k], factor) for k in range(3)]
    ).astype(jnp.bfloat16)
    grad_two = lax.psum(
        lax.psum_scatter(part_two, "dp", scatter_dimension=2, tiled=True).astype(jnp.float32), "seq"
    )
    grad_later = shifted(middle_gradient, "seq", -2)
    grad_earlier = shifted(middle_gradient, "seq", 2)
    first_layer_taps = (grad_later, middle_gradient, grad_earlier)
    delta_zero = back_product(first_layer_taps[0], full_one[0])
    delta_zero = delta_zero + back_product(first_layer_taps[1], full_one[1])
    delta_zero = delta_zero + back_product(first_layer_taps[2], full_one[2])
    input_grad = (middle_gradient.astype(jnp.float32) + gelu_slope(inputs_f) * delta_zero).astype(
        jnp.bfloat16
    )
    part_one = jnp.stack(
        [outer_terms(input_activation, first_layer_taps[k], factor) for k in range(3)]
    ).astype(jnp.bfloat16)
    grad_one = lax.psum(
        lax.psum_scatter(part_one, "dp", scatter_dimension=2, tiled=True).astype(jnp.float32), "seq"
    )
    return (input_grad.reshape(inputs.shape), grad_one, grad_two)


def pack(left, right):
    cut = right.shape[1] // 128 * 128
    return jnp.concatenate([left, right[:, cut:], right[:, :cut]], axis=1)


def unpack(both):
    chans = both.shape[1] // 2
    rest = chans % 128
    right = jnp.concatenate([both[:, chans + rest :], both[:, chans : chans + rest]], axis=1)
    return both[:, :chans], right


def gelu_and_slope(value):
    inner = math.sqrt(2.0 / math.pi)
    square = value * value
    bend = jnp.tanh(inner * value * (1.0 + 0.044715 * square))
    half = 0.5 * (1.0 + bend)
    slope = half + 0.5 * value * (1.0 - bend * bend) * (inner * (1.0 + 3.0 * 0.044715 * square))
    return value * half, slope


def product(left, right):
    return jnp.dot(left, right, preferred_element_type=jnp.float32)


def outer(left, right):
    return lax.dot_general(
        left, right, (((1,), (1,)), ((), ())), preferred_element_type=jnp.float32
    )


def pair_kernel(
    factor,
    x_ref, c_ref, w1_ref, w2_ref,
    ig_ref, g_one_ref, g_two_ref,
    sums, xs, retb, igs, taps, wts, wt, wn, terms,
    s_core, r_core, s_chip, r_chip, acc, s_near, r_near, s_far, r_far, s_last, r_last,
    xs_send, xs_recv, own_sem, tap_sem, ret_send, ret_recv, w_send, w_recv, red_send, red_recv,
):
    f32, bf16 = jnp.float32, jnp.bfloat16
    chans, positions = x_ref.shape
    half = positions // 2
    size = half // CHUNKS
    width = wts.shape[1]
    z, d = lax.axis_index("seq"), lax.axis_index("dp")
    role = z // 2
    other = 1 - role
    far = lax.rem(z + 2, 4)
    parity = lax.rem(z, 2)
    near = z + 1 - 2 * parity
    core = lax.rem(d, 2)
    chip = d // 2
    sibling = d + 1 - 2 * core
    across = lax.rem(d + 2, 4)

    barrier = pltpu.get_barrier_semaphore()
    for axis, peer in (("seq", far), ("seq", near), ("dp", sibling), ("dp", across)):
        pl.semaphore_signal(barrier, inc=1, device_id={axis: peer}, device_id_type=MESH)

    own_half = pl.ds(pl.multiple_of(role * half, 128), half)
    own_copies = [
        pltpu.make_async_copy(ref.at[:, own_half], xs.at[role, i], own_sem.at[i])
        for i, ref in enumerate((x_ref, c_ref))
    ]
    tap_copies = [
        pltpu.make_async_copy(w1_ref, taps.at[pl.ds(0, 3)], tap_sem.at[0]),
        pltpu.make_async_copy(w2_ref.at[1], taps.at[3], tap_sem.at[1]),
    ]

    def columns(start, count):
        return pl.ds(pl.multiple_of(start, 128), count)

    def owned_rows(owner):
        return pl.ds(pl.multiple_of(owner * width, 16), width)

    def remote(src, dst, send, recv, axis, peer):
        return pltpu.make_async_remote_copy(
            src_ref=src, dst_ref=dst, send_sem=send, recv_sem=recv,
            device_id={axis: peer}, device_id_type=MESH,
        )

    def move(ch):
        return [
            remote(
                ref.at[:, columns(other * half + ch * size, size)],
                xs.at[role, i, :, columns(ch * size, size)],
                xs_send.at[ch, i], xs_recv.at[ch, i], "seq", far,
            )
            for i, ref in enumerate((x_ref, c_ref))
        ]

    def give_back(ch):
        return remote(
            retb.at[:, columns(ch * size, size)],
            ig_ref.at[:, columns(role * half + ch * size, size)],
            ret_send.at[ch], ret_recv.at[ch], "seq", far,
        )

    for copy in tap_copies:
        copy.start()
    pl.semaphore_wait(barrier, 4)
    for ch in range(AHEAD):
        for copy in move(ch):
            copy.start()
    for copy in own_copies:
        copy.start()

    for copy in tap_copies:
        copy.wait()
    for k in range(4):
        turned = taps[k].astype(f32).T.astype(bf16)
        wts[k] = turned
        wt[k, owned_rows(d), :] = turned
    shares = [
        remote(
            wts, wt.at[:, owned_rows(d)], w_send.at[j], w_recv.at[j], "dp", peer
        )
        for j, peer in enumerate((across, sibling))
    ]
    for copy in shares:
        copy.start()
    terms[...] = jnp.zeros_like(terms)
    shares[0].wait_recv()
    arrived = wt.at[:, owned_rows(across)]
    passed = remote(arrived, arrived, w_send.at[2], w_recv.at[2], "dp", sibling)
    passed.start()
    shares[1].wait_recv()
    passed.wait_recv()
    for k in range(4):
        wn[k] = wt[k].astype(f32).T.astype(bf16)
    for copy in own_copies:
        copy.wait()

    def work(ch, carry):
        for copy in move(ch):
            copy.wait_recv()

        @pl.when(ch + AHEAD < CHUNKS)
        def _():
            for copy in move(ch + AHEAD):
                copy.start()

        @pl.when(ch == CHUNKS - 2)
        def _():
            for early in range(CHUNKS - 3):
                give_back(early).start()

        @pl.when(ch == CHUNKS - 1)
        def _():
            for early in range(CHUNKS - 3, CHUNKS - 1):
                give_back(early).start()

        piece = columns(ch * size, size)
        x_f = jnp.concatenate([xs[0, 0, :, piece], xs[1, 0, :, piece]], axis=1).astype(f32)
        c_b = jnp.concatenate([xs[0, 1, :, piece], xs[1, 1, :, piece]], axis=1)
        act, slope_x = gelu_and_slope(x_f)
        act = act.astype(bf16)
        low, high = act[:, :size], act[:, size:]
        cross = jnp.concatenate([product(wt[2], high), product(wt[0], low)], axis=1)
        hidden = (x_f + (product(wt[1], act) + cross)).astype(bf16).astype(f32)
        act_one, slope_h = gelu_and_slope(hidden)
        act_one = act_one.astype(bf16)
        grad_mid = (c_b.astype(f32) + slope_h * product(wn[3], c_b)).astype(bf16)
        g_low, g_high = grad_mid[:, :size], grad_mid[:, size:]
        terms[3] += outer(c_b, act_one)
        terms[0] += outer(g_high, low)
        terms[1] += outer(grad_mid, act)
        terms[2] += outer(g_low, high)
        cross = jnp.concatenate([product(wn[0], g_high), product(wn[2], g_low)], axis=1)
        delta = product(wn[1], grad_mid) + cross
        result = (grad_mid.astype(f32) + slope_x * delta).astype(bf16)
        igs[0] = result[:, :size]
        igs[1] = result[:, size:]
        ig_ref[:, columns(role * half + ch * size, size)] = igs[role]
        retb[:, piece] = igs[other]
        return carry

    lax.fori_loop(0, CHUNKS, work, 0)

    steps = [(0, 48), (48, 32), (80, 32)] if width == 112 else [(0, width)]

    def slice_of(owner, start, count):
        owned = pl.ds(pl.multiple_of(owner * width + start, 16), count)
        own = [terms[k, owned, :] * factor for k in range(4)]
        return pack(own[0], own[1]), pack(own[2], own[3])

    def reduce_copy(kind, q, src, dst, axis, peer):
        return remote(src, dst, red_send.at[kind, q], red_recv.at[kind, q], axis, peer)

    copies = [[], [], [], [], [], []]
    for j, for_chip in enumerate((1 - chip, chip)):
        for q, (start, count) in enumerate(steps):
            span = pl.ds(start, count)
            for p, part in enumerate(slice_of(2 * for_chip + 1 - core, start, count)):
                s_core[j, p, span, :] = part.astype(bf16)
            copies[j].append(
                reduce_copy(
                    j, q, s_core.at[j, :, span], r_core.at[j, :, span], "dp", sibling
                )
            )
            copies[j][q].start()
    for q, (start, count) in enumerate(steps):
        span = pl.ds(start, count)
        copies[0][q].wait_recv()
        for p, part in enumerate(slice_of(2 * (1 - chip) + core, start, count)):
            s_chip[p, span, :] = (part + r_core[0, p, span, :].astype(f32)).astype(bf16)
        copies[2].append(
            reduce_copy(2, q, s_chip.at[:, span], r_chip.at[:, span], "dp", across)
        )
        copies[2][q].start()
    for q, (start, count) in enumerate(steps):
        span = pl.ds(start, count)
        copies[1][q].wait_recv()
        for p, part in enumerate(slice_of(d, start, count)):
            acc[p, span, :] = part + r_core[1, p, span, :].astype(f32)
    for q, (start, count) in enumerate(steps):
        span = pl.ds(start, count)
        copies[2][q].wait_recv()
        for p in range(2):
            acc[p, span, :] += r_chip[p, span, :].astype(f32)
        s_near[span, :] = acc[1 - parity, span, :].astype(bf16)
        copies[3].append(reduce_copy(3, q, s_near.at[span], r_near.at[span], "seq", near))
        copies[3][q].start()
    for q, (start, count) in enumerate(steps):
        span = pl.ds(start, count)
        copies[3][q].wait_recv()
        s_far[span, :] = (acc[parity, span, :] + r_near[span, :].astype(f32)).astype(bf16)
        copies[4].append(reduce_copy(4, q, s_far.at[span], r_far.at[span], "seq", far))
        copies[4][q].start()
    give_back(CHUNKS - 1).start()
    outside = jnp.zeros((chans, width), f32)
    g_two_ref[0] = outside
    g_two_ref[2] = outside
    for q, (start, count) in enumerate(steps):
        span = pl.ds(start, count)
        copies[4][q].wait_recv()
        total = (s_far[span, :].astype(f32) + r_far[span, :].astype(f32)).astype(bf16)
        s_last[span, :] = total
        copies[5].append(reduce_copy(5, q, s_last.at[span], r_last.at[span], "seq", near))
        copies[5][q].start()
        for i, part in enumerate(unpack(total.astype(f32))):
            sums[2 * parity + i, span, :] = part
    for q, (start, count) in enumerate(steps):
        span = pl.ds(start, count)
        copies[5][q].wait_recv()
        for i, part in enumerate(unpack(r_last[span, :].astype(f32))):
            sums[2 * (1 - parity) + i, span, :] = part
    for k in range(3):
        g_one_ref[k] = sums[k].T
    g_two_ref[1] = sums[3].T

    for ch in range(CHUNKS):
        give_back(ch).wait()
        for copy in move(ch):
            copy.wait_send()
    for group in (shares, [passed], *copies):
        for copy in group:
            copy.wait_send()


def pair_plan(inputs, cotangent, first_weight_matrix, weight_two):
    positions, chans = inputs.shape[1:]
    width = first_weight_matrix.shape[2]
    factor = 1.0 / math.sqrt(
        lax.axis_size("dp") * positions * lax.axis_size("seq")
    )
    half = positions // 2
    f32, bf16 = jnp.float32, jnp.bfloat16
    vmem = pl.BlockSpec(memory_space=pltpu.VMEM)
    hbm = pl.BlockSpec(memory_space=pltpu.HBM)
    dma = pltpu.SemaphoreType.DMA
    packed = (width, 2 * chans)
    result, grad_one, grad_two = pl.pallas_call(
        functools.partial(pair_kernel, factor),
        out_shape=(
            jax.ShapeDtypeStruct((chans, positions), bf16),
            jax.ShapeDtypeStruct((3, chans, width), f32),
            jax.ShapeDtypeStruct((3, chans, width), f32),
        ),
        in_specs=[hbm] * 4,
        out_specs=(vmem, vmem, vmem),
        scratch_shapes=[
            pltpu.VMEM((4, width, chans), f32),
            pltpu.VMEM((2, 2, chans, half), bf16),
            pltpu.VMEM((chans, half), bf16),
            pltpu.VMEM((2, chans, half // CHUNKS), bf16),
            pltpu.VMEM((4, chans, width), bf16),
            pltpu.VMEM((4, width, chans), bf16),
            pltpu.VMEM((4, chans, chans), bf16),
            pltpu.VMEM((4, chans, chans), bf16),
            pltpu.VMEM((4, chans, chans), f32),
            pltpu.VMEM((2, 2, *packed), bf16),
            pltpu.VMEM((2, 2, *packed), bf16),
            pltpu.VMEM((2, *packed), bf16),
            pltpu.VMEM((2, *packed), bf16),
            pltpu.VMEM((2, *packed), f32),
            *[pltpu.VMEM(packed, bf16)] * 6,
            dma((CHUNKS, 2)), dma((CHUNKS, 2)), dma((2,)), dma((2,)),
            dma((CHUNKS,)), dma((CHUNKS,)), dma((3,)), dma((3,)), dma((6, 3)), dma((6, 3)),
        ],
        compiler_params=pltpu.CompilerParams(
            collective_id=0, has_side_effects=True, vmem_limit_bytes=62 * 2**20
        ),
    )(inputs[0].T, cotangent[0].T, first_weight_matrix, weight_two)
    return result.T[None], grad_one, grad_two


def on_device(inputs, cotangent, first_weight_matrix, weight_two):
    sequences, positions, chans = inputs.shape
    length = positions * lax.axis_size("seq")
    paired = lax.axis_size("seq") == 4 and lax.axis_size("dp") == 4 and sequences == 1
    if paired and length == 2 * FIRST_SPACING and length <= SECOND_SPACING:
        return pair_plan(inputs, cotangent, first_weight_matrix, weight_two)
    return spread_plan(inputs, cotangent, first_weight_matrix, weight_two)


def solution(mesh):
    placed = (
        P(("groups", "dp"), "seq", None),
        P(("groups", "dp"), "seq", None),
        P(None, None, "dp"),
        P(None, None, "dp"),
    )
    return jax.shard_map(
        on_device,
        mesh=mesh,
        in_specs=placed,
        out_specs=(
            P(("groups", "dp"), "seq", None),
            P("groups", None, "dp"),
            P("groups", None, "dp"),
        ),
        check_vma=False,
    )
```

```python
import functools
import math

import jax
import jax.numpy as jnp
from jax import lax
from jax.experimental import pallas as pl
from jax.experimental.pallas import tpu as pltpu
from jax.sharding import PartitionSpec as P


MESH = pl.DeviceIdType.MESH
FIRST_SPACING = 2048
SECOND_SPACING = 4096
CHUNKS = 4
AHEAD = 2


def shifted(block, axis, distance):
    devices = range(lax.axis_size(axis))
    route = [(i - distance, i) for i in devices if i - distance in devices]
    return lax.ppermute(block, axis, route)


def gelu_slope(value):
    return jax.vjp(jax.nn.gelu, value)[1](jnp.ones_like(value))[0]


def outer_terms(left, right, factor):
    product = lax.dot_general(
        left, right, (((0,), (0,)), ((), ())), preferred_element_type=jnp.float32
    )
    return product * factor


def back_product(tap, weight):
    return lax.dot_general(
        tap, weight, (((1,), (1,)), ((), ())), preferred_element_type=jnp.float32
    )


def spread_plan(inputs, cotangent, first_weight_matrix, weight_two):
    chans = inputs.shape[2]
    rows = inputs.shape[0] * inputs.shape[1]
    factor = 1.0 / math.sqrt(
        inputs.shape[0] * lax.axis_size("dp") * inputs.shape[1] * lax.axis_size("seq")
    )
    full_one = lax.all_gather(first_weight_matrix, "dp", axis=2, tiled=True)
    flat_in = inputs.reshape(rows, chans)
    inputs_f = flat_in.astype(jnp.float32)
    input_activation = jax.nn.gelu(inputs_f).astype(jnp.bfloat16)
    act_before = shifted(input_activation, "seq", 2)
    act_after = shifted(input_activation, "seq", -2)
    flat_cot = cotangent.reshape(rows, chans)
    cot_later = shifted(flat_cot, "seq", -4)
    cot_earlier = shifted(flat_cot, "seq", 4)
    preactivation = jnp.dot(act_before, full_one[0], preferred_element_type=jnp.float32)
    preactivation = preactivation + jnp.dot(
        input_activation, full_one[1], preferred_element_type=jnp.float32
    )
    preactivation = preactivation + jnp.dot(
        act_after, full_one[2], preferred_element_type=jnp.float32
    )
    hidden_f = (inputs_f + preactivation).astype(jnp.bfloat16).astype(jnp.float32)
    act_one = jax.nn.gelu(hidden_f).astype(jnp.bfloat16)
    full_two = lax.all_gather(weight_two, "dp", axis=2, tiled=True)
    second_layer_taps = (cot_later, flat_cot, cot_earlier)
    delta_one = back_product(second_layer_taps[0], full_two[0])
    delta_one = delta_one + back_product(second_layer_taps[1], full_two[1])
    delta_one = delta_one + back_product(second_layer_taps[2], full_two[2])
    middle_gradient = (flat_cot.astype(jnp.float32) + gelu_slope(hidden_f) * delta_one).astype(
        jnp.bfloat16
    )
    part_two = jnp.stack(
        [outer_terms(act_one, second_layer_taps[k], factor) for k in range(3)]
    ).astype(jnp.bfloat16)
    grad_two = lax.psum(
        lax.psum_scatter(part_two, "dp", scatter_dimension=2, tiled=True).astype(jnp.float32), "seq"
    )
    grad_later = shifted(middle_gradient, "seq", -2)
    grad_earlier = shifted(middle_gradient, "seq", 2)
    first_layer_taps = (grad_later, middle_gradient, grad_earlier)
    delta_zero = back_product(first_layer_taps[0], full_one[0])
    delta_zero = delta_zero + back_product(first_layer_taps[1], full_one[1])
    delta_zero = delta_zero + back_product(first_layer_taps[2], full_one[2])
    input_grad = (middle_gradient.astype(jnp.float32) + gelu_slope(inputs_f) * delta_zero).astype(
        jnp.bfloat16
    )
    part_one = jnp.stack(
        [outer_terms(input_activation, first_layer_taps[k], factor) for k in range(3)]
    ).astype(jnp.bfloat16)
    grad_one = lax.psum(
        lax.psum_scatter(part_one, "dp", scatter_dimension=2, tiled=True).astype(jnp.float32), "seq"
    )
    return (input_grad.reshape(inputs.shape), grad_one, grad_two)


def pack(left, right):
    cut = right.shape[1] // 128 * 128
    return jnp.concatenate([left, right[:, cut:], right[:, :cut]], axis=1)


def unpack(both):
    chans = both.shape[1] // 2
    rest = chans % 128
    right = jnp.concatenate([both[:, chans + rest :], both[:, chans : chans + rest]], axis=1)
    return both[:, :chans], right


def gelu_and_slope(value):
    inner = math.sqrt(2.0 / math.pi)
    square = value * value
    bend = jnp.tanh(inner * value * (1.0 + 0.044715 * square))
    half = 0.5 * (1.0 + bend)
    slope = half + 0.5 * value * (1.0 - bend * bend) * (inner * (1.0 + 3.0 * 0.044715 * square))
    return value * half, slope


def product(left, right):
    return jnp.dot(left, right, preferred_element_type=jnp.float32)


def outer(left, right):
    return lax.dot_general(
        left, right, (((1,), (1,)), ((), ())), preferred_element_type=jnp.float32
    )


def pair_kernel(
    factor,
    x_ref, c_ref, w1_ref, w2_ref,
    ig_ref, g_one_ref, g_two_ref,
    sums, xs, retb, igs, taps, wts, wt, wn, terms,
    s_core, r_core, s_chip, r_chip, acc, s_near, r_near, s_far, r_far, s_last, r_last,
    xs_send, xs_recv, own_sem, tap_sem, ret_send, ret_recv, w_send, w_recv, red_send, red_recv,
):
    f32, bf16 = jnp.float32, jnp.bfloat16
    chans, positions = x_ref.shape
    half = positions // 2
    size = half // CHUNKS
    width = wts.shape[1]
    z, d = lax.axis_index("seq"), lax.axis_index("dp")
    role = z // 2
    other = 1 - role
    far = lax.rem(z + 2, 4)
    parity = lax.rem(z, 2)
    near = z + 1 - 2 * parity
    core = lax.rem(d, 2)
    chip = d // 2
    sibling = d + 1 - 2 * core
    across = lax.rem(d + 2, 4)

    barrier = pltpu.get_barrier_semaphore()
    for axis, peer in (("seq", far), ("seq", near), ("dp", sibling), ("dp", across)):
        pl.semaphore_signal(barrier, inc=1, device_id={axis: peer}, device_id_type=MESH)

    own_half = pl.ds(pl.multiple_of(role * half, 128), half)
    own_copies = [
        pltpu.make_async_copy(ref.at[:, own_half], xs.at[role, i], own_sem.at[i])
        for i, ref in enumerate((x_ref, c_ref))
    ]
    tap_copies = [
        pltpu.make_async_copy(w1_ref, taps.at[pl.ds(0, 3)], tap_sem.at[0]),
        pltpu.make_async_copy(w2_ref.at[1], taps.at[3], tap_sem.at[1]),
    ]

    def columns(start, count):
        return pl.ds(pl.multiple_of(start, 128), count)

    def owned_rows(owner):
        return pl.ds(pl.multiple_of(owner * width, 16), width)

    def remote(src, dst, send, recv, axis, peer):
        return pltpu.make_async_remote_copy(
            src_ref=src, dst_ref=dst, send_sem=send, recv_sem=recv,
            device_id={axis: peer}, device_id_type=MESH,
        )

    def move(ch):
        return [
            remote(
                ref.at[:, columns(other * half + ch * size, size)],
                xs.at[role, i, :, columns(ch * size, size)],
                xs_send.at[ch, i], xs_recv.at[ch, i], "seq", far,
            )
            for i, ref in enumerate((x_ref, c_ref))
        ]

    def give_back(ch):
        return remote(
            retb.at[:, columns(ch * size, size)],
            ig_ref.at[:, columns(role * half + ch * size, size)],
            ret_send.at[ch], ret_recv.at[ch], "seq", far,
        )

    for copy in tap_copies:
        copy.start()
    pl.semaphore_wait(barrier, 4)
    for ch in range(AHEAD):
        for copy in move(ch):
            copy.start()
    for copy in own_copies:
        copy.start()

    for copy in tap_copies:
        copy.wait()
    for k in range(4):
        turned = taps[k].astype(f32).T.astype(bf16)
        wts[k] = turned
        wt[k, owned_rows(d), :] = turned
    shares = [
        remote(
            wts, wt.at[:, owned_rows(d)], w_send.at[j], w_recv.at[j], "dp", peer
        )
        for j, peer in enumerate((across, sibling))
    ]
    for copy in shares:
        copy.start()
    terms[...] = jnp.zeros_like(terms)
    shares[0].wait_recv()
    arrived = wt.at[:, owned_rows(across)]
    passed = remote(arrived, arrived, w_send.at[2], w_recv.at[2], "dp", sibling)
    passed.start()
    shares[1].wait_recv()
    passed.wait_recv()
    for k in range(4):
        wn[k] = wt[k].astype(f32).T.astype(bf16)
    for copy in own_copies:
        copy.wait()

    def work(ch, carry):
        for copy in move(ch):
            copy.wait_recv()

        @pl.when(ch + AHEAD < CHUNKS)
        def _():
            for copy in move(ch + AHEAD):
                copy.start()

        @pl.when(ch == CHUNKS - 1)
        def _():
            for early in range(CHUNKS - 1):
                give_back(early).start()

        piece = columns(ch * size, size)
        x_f = jnp.concatenate([xs[0, 0, :, piece], xs[1, 0, :, piece]], axis=1).astype(f32)
        c_b = jnp.concatenate([xs[0, 1, :, piece], xs[1, 1, :, piece]], axis=1)
        act, slope_x = gelu_and_slope(x_f)
        act = act.astype(bf16)
        low, high = act[:, :size], act[:, size:]
        cross = jnp.concatenate([product(wt[2], high), product(wt[0], low)], axis=1)
        hidden = (x_f + (product(wt[1], act) + cross)).astype(bf16).astype(f32)
        act_one, slope_h = gelu_and_slope(hidden)
        act_one = act_one.astype(bf16)
        grad_mid = (c_b.astype(f32) + slope_h * product(wn[3], c_b)).astype(bf16)
        g_low, g_high = grad_mid[:, :size], grad_mid[:, size:]
        terms[3] += outer(c_b, act_one)
        terms[0] += outer(g_high, low)
        terms[1] += outer(grad_mid, act)
        terms[2] += outer(g_low, high)
        cross = jnp.concatenate([product(wn[0], g_high), product(wn[2], g_low)], axis=1)
        delta = product(wn[1], grad_mid) + cross
        result = (grad_mid.astype(f32) + slope_x * delta).astype(bf16)
        igs[0] = result[:, :size]
        igs[1] = result[:, size:]
        ig_ref[:, columns(role * half + ch * size, size)] = igs[role]
        retb[:, piece] = igs[other]
        return carry

    lax.fori_loop(0, CHUNKS, work, 0)

    steps = [(0, 64), (64, 48)] if width == 112 else [(0, width)]

    def slice_of(owner, start, count):
        owned = pl.ds(pl.multiple_of(owner * width + start, 16), count)
        own = [terms[k, owned, :] * factor for k in range(4)]
        return pack(own[0], own[1]), pack(own[2], own[3])

    def reduce_copy(kind, q, src, dst, axis, peer):
        return remote(src, dst, red_send.at[kind, q], red_recv.at[kind, q], axis, peer)

    copies = [[], [], [], [], [], []]
    for j, for_chip in enumerate((1 - chip, chip)):
        for q, (start, count) in enumerate(steps):
            span = pl.ds(start, count)
            for p, part in enumerate(slice_of(2 * for_chip + 1 - core, start, count)):
                s_core[j, p, span, :] = part.astype(bf16)
            copies[j].append(
                reduce_copy(
                    j, q, s_core.at[j, :, span], r_core.at[j, :, span], "dp", sibling
                )
            )
            copies[j][q].start()
    for q, (start, count) in enumerate(steps):
        span = pl.ds(start, count)
        copies[0][q].wait_recv()
        for p, part in enumerate(slice_of(2 * (1 - chip) + core, start, count)):
            s_chip[p, span, :] = (part + r_core[0, p, span, :].astype(f32)).astype(bf16)
        copies[2].append(
            reduce_copy(2, q, s_chip.at[:, span], r_chip.at[:, span], "dp", across)
        )
        copies[2][q].start()
    for q, (start, count) in enumerate(steps):
        span = pl.ds(start, count)
        copies[1][q].wait_recv()
        for p, part in enumerate(slice_of(d, start, count)):
            acc[p, span, :] = part + r_core[1, p, span, :].astype(f32)
    for q, (start, count) in enumerate(steps):
        span = pl.ds(start, count)
        copies[2][q].wait_recv()
        for p in range(2):
            acc[p, span, :] += r_chip[p, span, :].astype(f32)
        s_near[span, :] = acc[1 - parity, span, :].astype(bf16)
        copies[3].append(reduce_copy(3, q, s_near.at[span], r_near.at[span], "seq", near))
        copies[3][q].start()
    for q, (start, count) in enumerate(steps):
        span = pl.ds(start, count)
        copies[3][q].wait_recv()
        s_far[span, :] = (acc[parity, span, :] + r_near[span, :].astype(f32)).astype(bf16)
        copies[4].append(reduce_copy(4, q, s_far.at[span], r_far.at[span], "seq", far))
        copies[4][q].start()
    give_back(CHUNKS - 1).start()
    outside = jnp.zeros((width, chans), f32)
    g_two_ref[0] = outside
    g_two_ref[2] = outside
    for q, (start, count) in enumerate(steps):
        span = pl.ds(start, count)
        copies[4][q].wait_recv()
        total = (s_far[span, :].astype(f32) + r_far[span, :].astype(f32)).astype(bf16)
        s_last[span, :] = total
        copies[5].append(reduce_copy(5, q, s_last.at[span], r_last.at[span], "seq", near))
        copies[5][q].start()
        for i, part in enumerate(unpack(total.astype(f32))):
            sums[2 * parity + i, span, :] = part
    for q, (start, count) in enumerate(steps):
        span = pl.ds(start, count)
        copies[5][q].wait_recv()
        for i, part in enumerate(unpack(r_last[span, :].astype(f32))):
            sums[2 * (1 - parity) + i, span, :] = part
        for k in range(3):
            g_one_ref[k, span, :] = sums[k, span, :]
        g_two_ref[1, span, :] = sums[3, span, :]

    for ch in range(CHUNKS):
        give_back(ch).wait()
        for copy in move(ch):
            copy.wait_send()
    for group in (shares, [passed], *copies):
        for copy in group:
            copy.wait_send()


def pair_plan(inputs, cotangent, first_weight_matrix, weight_two):
    positions, chans = inputs.shape[1:]
    width = first_weight_matrix.shape[2]
    factor = 1.0 / math.sqrt(
        lax.axis_size("dp") * positions * lax.axis_size("seq")
    )
    half = positions // 2
    f32, bf16 = jnp.float32, jnp.bfloat16
    vmem = pl.BlockSpec(memory_space=pltpu.VMEM)
    hbm = pl.BlockSpec(memory_space=pltpu.HBM)
    dma = pltpu.SemaphoreType.DMA
    packed = (width, 2 * chans)
    result, grad_one, grad_two = pl.pallas_call(
        functools.partial(pair_kernel, factor),
        out_shape=(
            jax.ShapeDtypeStruct((chans, positions), bf16),
            jax.ShapeDtypeStruct((3, width, chans), f32),
            jax.ShapeDtypeStruct((3, width, chans), f32),
        ),
        in_specs=[hbm] * 4,
        out_specs=(vmem, vmem, vmem),
        scratch_shapes=[
            pltpu.VMEM((4, width, chans), f32),
            pltpu.VMEM((2, 2, chans, half), bf16),
            pltpu.VMEM((chans, half), bf16),
            pltpu.VMEM((2, chans, half // CHUNKS), bf16),
            pltpu.VMEM((4, chans, width), bf16),
            pltpu.VMEM((4, width, chans), bf16),
            pltpu.VMEM((4, chans, chans), bf16),
            pltpu.VMEM((4, chans, chans), bf16),
            pltpu.VMEM((4, chans, chans), f32),
            pltpu.VMEM((2, 2, *packed), bf16),
            pltpu.VMEM((2, 2, *packed), bf16),
            pltpu.VMEM((2, *packed), bf16),
            pltpu.VMEM((2, *packed), bf16),
            pltpu.VMEM((2, *packed), f32),
            *[pltpu.VMEM(packed, bf16)] * 6,
            dma((CHUNKS, 2)), dma((CHUNKS, 2)), dma((2,)), dma((2,)),
            dma((CHUNKS,)), dma((CHUNKS,)), dma((3,)), dma((3,)), dma((6, 3)), dma((6, 3)),
        ],
        compiler_params=pltpu.CompilerParams(
            collective_id=0, has_side_effects=True, vmem_limit_bytes=62 * 2**20
        ),
    )(inputs[0].T, cotangent[0].T, first_weight_matrix, weight_two)
    return result.T[None], grad_one.transpose(0, 2, 1), grad_two.transpose(0, 2, 1)


def on_device(inputs, cotangent, first_weight_matrix, weight_two):
    sequences, positions, chans = inputs.shape
    length = positions * lax.axis_size("seq")
    paired = lax.axis_size("seq") == 4 and lax.axis_size("dp") == 4 and sequences == 1
    if paired and length == 2 * FIRST_SPACING and length <= SECOND_SPACING:
        return pair_plan(inputs, cotangent, first_weight_matrix, weight_two)
    return spread_plan(inputs, cotangent, first_weight_matrix, weight_two)


def solution(mesh):
    placed = (
        P(("groups", "dp"), "seq", None),
        P(("groups", "dp"), "seq", None),
        P(None, None, "dp"),
        P(None, None, "dp"),
    )
    return jax.shard_map(
        on_device,
        mesh=mesh,
        in_specs=placed,
        out_specs=(
            P(("groups", "dp"), "seq", None),
            P("groups", None, "dp"),
            P("groups", None, "dp"),
        ),
        check_vma=False,
    )
```
